256 devices in a mesh: src: 32 (over x_lo, z, core), tgt: 8 (over x_hi, y).
Axes of the slice: x: 4 (x_hi: 2, x_lo: 2; x = x_hi * 2 + x_lo), y: 4, z: 8, core: 2. Of those that a mesh axis runs over, the one named last changes fastest.
Arguments:
- weights_in: bfloat16 [4, 32768, 32, 128], P(None, ('src', 'tgt')), may hold values from -6 to 6
- twiddles: float32 [4, 4, 32768, 128], P(None, None, ('src', 'tgt')), may hold values from -1 to 1, as said below
- kernels: bfloat16 [3, 2, 2, 128, 128], replicated, may hold values from -1 to 1
Outputs:
- weights_out: bfloat16 [4, 32768, 32, 128], P(None, ('src', 'tgt'))
The draws below stay inside these ranges and needn't reach their ends.
Inputs may be any that keep to these rules, and one draw needn't show every extreme that they name: `twiddles`: entries j and j + 64 of each twiddle row are the cosine and sine of one angle.
All inputs are finite; a program needn't handle non-finite values.
Results may differ from the reference program's by a relative error of at most 0.018.
Values may be sent and summed in bfloat16 or wider, within the bound.
No kernel may reach another device: no remote copies, remote signals or barrier semaphores. Data moves between devices by JAX's collectives and lax.ppermute only.
A program may use at most 64 MiB of HBM per device.

```python
import math
import jax
import jax.numpy as jnp
from jax import lax

R = 64
LAWS = 32
LEV = 3
NA = 4
NB = 32768
FAR_GAP = 16384
NEAR_GAP = 8192
MIRROR_GAP = 512


def draw_twiddles(key, part):
    key = jax.random.fold_in(key, 11)
    angles = jax.random.uniform(key, (LEV + 1, NA, NB, R), jnp.float32, -math.pi, math.pi)
    return jnp.concatenate([jnp.cos(angles), jnp.sin(angles)], -1)


def draw_kernels(key, part):
    key = jax.random.fold_in(key, 23)
    span_width = 2 * R
    noise_part = jnp.clip(jax.random.normal(key, (LEV, 2, 2, span_width, span_width), jnp.float32), -6.0, 6.0)
    identity = jnp.eye(span_width, dtype=jnp.float32)
    return (0.5 * identity + 0.5 * noise_part / math.sqrt(span_width)).astype(jnp.bfloat16)


def block_scale(key, extent, shards, smallest, top_value):
    loudness, own = 1.0, jax.random.fold_in(key, 6)
    for dim, shards_of in shards:
        steps = jnp.exp(jax.random.uniform(jax.random.fold_in(own, dim), (shards_of,), jnp.float32, smallest / len(shards), top_value / len(shards)))
        loudness = loudness * jnp.repeat(steps, extent[dim] // shards_of).reshape([-1 if axis == dim else 1 for axis in range(len(extent))])
    return loudness


def gaussian(rng, extent, deviation, limit, cuts=(), kind=jnp.bfloat16):
    values = deviation * jax.random.normal(rng, extent, jnp.float32)
    if cuts:
        values = values * block_scale(rng, extent, cuts, -0.22, 0.18)
    return jnp.clip(values, -limit, limit).astype(kind)


def setup_inputs(seed: int = 0) -> dict:
    seeds = jax.random.split(jax.random.key(seed), 4)
    return {
        "weights_in": gaussian(seeds[0], (NA, NB, LAWS, 2 * R), 1.0, 6.0, ((1, 256),)),
        "twiddles": draw_twiddles(jax.random.fold_in(seeds[3], 71), 0),
        "kernels": draw_kernels(jax.random.fold_in(seeds[3], 71), 0),
    }


def rotate_phase(current, twiddle_row):
    half_width = twiddle_row.shape[-1] // 2
    cosine = twiddle_row[..., None, :half_width]
    sine_part = twiddle_row[..., None, half_width:]
    real_part = current[..., :half_width]
    imag_part = current[..., half_width:]
    return jnp.concatenate([cosine * real_part - sine_part * imag_part, sine_part * real_part + cosine * imag_part], -1)


def one_level(current, twiddle_row, kernel_pair, slot_gap):
    inputs = rotate_phase(current, twiddle_row).astype(jnp.bfloat16)
    slot_count = inputs.shape[0]
    grouped = inputs.reshape(slot_count // (2 * slot_gap), 2, slot_gap, inputs.shape[1], inputs.shape[2])
    merged = jnp.einsum("hsglm,csmn->hcgln", grouped.astype(jnp.float32), kernel_pair.astype(jnp.float32))
    return merged.reshape(slot_count, inputs.shape[1], inputs.shape[2])


def reference(weights_in, twiddles, kernels):
    per_target = jnp.moveaxis(twiddles, 1, 0)
    gaps = (FAR_GAP, NEAR_GAP, MIRROR_GAP)

    def one_target(pair):
        current, rows = pair
        for level_index in range(3):
            current = one_level(current, rows[level_index], kernels[level_index], gaps[level_index])
        return rotate_phase(current, rows[3]).astype(jnp.bfloat16)

    return lax.map(one_target, (weights_in, per_target))
```

```python
import functools

import jax
import jax.numpy as jnp
from jax import lax
from jax.experimental import pallas as pl
from jax.experimental.pallas import tpu as pltpu
from jax.sharding import PartitionSpec as P

FIRST, SECOND, THIRD = 4, 2, 1
GATHERED = 2
TILE = 32
VMEM = 48 * 2**20


def swap(block, mask):
    n_src, n_tgt = lax.axis_size("src"), lax.axis_size("tgt")
    flip_src = (n_src // 2 if mask & FIRST else 0) + (n_src // 4 if mask & SECOND else 0)
    flip_tgt = n_tgt // 2 if mask & THIRD else 0
    if not flip_tgt:
        return lax.ppermute(block, "src", [(i, i ^ flip_src) for i in range(n_src)])
    if not flip_src:
        return lax.ppermute(block, "tgt", [(i, i ^ flip_tgt) for i in range(n_tgt)])
    route = []
    for i in range(n_src):
        for j in range(n_tgt):
            route.append((i * n_tgt + j, (i ^ flip_src) * n_tgt + (j ^ flip_tgt)))
    return lax.ppermute(block, ("src", "tgt"), route)


def my_order():
    n_src, n_tgt = lax.axis_size("src"), lax.axis_size("tgt")
    place = lax.axis_index("src") // (n_src // 4) * 2 + lax.axis_index("tgt") // (n_tgt // 2)
    return jnp.bitwise_xor(place.astype(jnp.int32), jnp.arange(8, dtype=jnp.int32))


def roll_half(block):
    return pltpu.roll(block, block.shape[-1] // 2, 1)


def phases(rows):
    turned = roll_half(rows)
    low = lax.broadcasted_iota(jnp.int32, rows.shape, 1) < rows.shape[-1] // 2
    return jnp.where(low, rows, turned)[:, None, :], jnp.where(low, -turned, rows)[:, None, :]


def twist(plain, turned, rows):
    co, si = phases(rows)
    shape = (rows.shape[0], plain.shape[0] // rows.shape[0], plain.shape[1])
    return (plain.reshape(shape) * co + turned.reshape(shape) * si).reshape(plain.shape)


def twist_16(block, rows):
    wide = block.astype(jnp.float32)
    return twist(wide, roll_half(wide), rows)


def call(kernel, out_shape, grid, in_specs, out_specs, args, order, scratch=(), aliases=None, flops=0, nbytes=0):
    return pl.pallas_call(
        kernel,
        out_shape=out_shape,
        grid_spec=pltpu.PrefetchScalarGridSpec(
            num_scalar_prefetch=1, grid=grid, in_specs=in_specs, out_specs=out_specs, scratch_shapes=list(scratch)
        ),
        input_output_aliases=aliases or {},
        compiler_params=pltpu.CompilerParams(vmem_limit_bytes=VMEM),
        cost_estimate=pl.CostEstimate(flops=flops, bytes_accessed=nbytes, transcendentals=0),
    )(order, *args)


def first_kernel(order, w, t, _, out):
    slots, laws, width = out.shape
    out[...] = twist_16(w[0].reshape(slots * laws, width), t[0, 0]).astype(out.dtype).reshape(out.shape)


def first_twist(order, weights, twiddles, target, after):
    _, slots, laws, width = weights.shape
    tile = min(TILE, slots)
    return call(
        first_kernel,
        jax.ShapeDtypeStruct((slots, laws, width), weights.dtype),
        (slots // tile,),
        [
            pl.BlockSpec((1, tile, laws, width), lambda i, o: (target, i, 0, 0)),
            pl.BlockSpec((1, 1, tile, width), lambda i, o: (0, target, i, 0)),
            pl.BlockSpec(memory_space=pl.ANY),
        ],
        pl.BlockSpec((tile, laws, width), lambda i, o: (i, 0, 0)),
        (weights, twiddles, after),
        order,
        nbytes=4 * slots * laws * width,
    )


def level_kernel(bit, order, own, other, maps, t, *rest):
    out, both = rest[-2], rest[-1]
    slots, laws, width = own.shape

    @pl.when(pl.program_id(0) == 0)
    def _():
        child = lax.div(order[0], bit) & 1
        for source in range(2):
            part = maps[0, child, child if source == 0 else 1 - child]
            both[source * width : (source + 1) * width, :width] = part
            turned = roll_half(part.astype(jnp.float32)).astype(part.dtype)
            both[source * width : (source + 1) * width, width:] = turned

    rows = slots * laws
    state = jnp.dot(own[...].reshape(rows, width), both[:width, :], preferred_element_type=jnp.float32)
    state += jnp.dot(other[...].reshape(rows, width), both[width:, :], preferred_element_type=jnp.float32)
    out[...] = twist(state[:, :width], state[:, width:], t[0, 0]).astype(out.dtype).reshape(out.shape)


def level(order, own, other, kernels, twiddles, index, bit, target, whole=None, last=False):
    slots, laws, width = own.shape
    tile = min(TILE, slots)
    block = pl.BlockSpec((tile, laws, width), lambda i, o: (i, 0, 0))
    in_specs = [
        block,
        block,
        pl.BlockSpec((1, 2, 2, width, width), lambda i, o: (index, 0, 0, 0, 0)),
        pl.BlockSpec((1, 1, tile, width), lambda i, o: (index + 1, target, i, 0)),
    ]
    args, aliases = [own, other, kernels, twiddles], {}
    out_shape, out_spec = jax.ShapeDtypeStruct(own.shape, own.dtype), block
    if last:
        out_shape = jax.ShapeDtypeStruct((twiddles.shape[1], *own.shape), own.dtype)
        out_spec = pl.BlockSpec((None, tile, laws, width), lambda i, o: (target, i, 0, 0))
        if whole is not None:
            args.append(whole)
            in_specs.append(pl.BlockSpec(memory_space=pl.ANY))
            aliases = {5: 0}
    return call(
        functools.partial(level_kernel, bit),
        out_shape,
        (slots // tile,),
        in_specs,
        out_spec,
        args,
        order,
        scratch=[pltpu.VMEM((2 * width, 2 * width), own.dtype)],
        aliases=aliases,
        flops=8 * slots * laws * width * width,
        nbytes=6 * slots * laws * width,
    )


PLANE = (0, THIRD, FIRST, FIRST | THIRD)


def pack_kernel(order, w, t, out):
    targets, slots, laws, width = w.shape
    rows = slots * laws
    for target in range(targets):
        block = twist_16(w[target].reshape(rows, width), t[0, target])
        out[0, target * rows : (target + 1) * rows, :] = block.astype(out.dtype)
        for later in range(2):
            start = targets * rows + (later * targets + target) * slots
            out[0, start : start + slots, :] = t[1 + later, target].astype(out.dtype)


def pack(order, weights, twiddles, far):
    _, slots, laws, width = weights.shape
    eighth = slots // 8
    rows = GATHERED * eighth * (laws + 2)

    def which(i, o):
        return o[lax.div(i, 2) * FIRST + lax.rem(i, 2) * THIRD + far]

    return call(
        pack_kernel,
        jax.ShapeDtypeStruct((4, rows, width), weights.dtype),
        (4,),
        [
            pl.BlockSpec((GATHERED, eighth, laws, width), lambda i, o: (0, which(i, o), 0, 0)),
            pl.BlockSpec((3, GATHERED, eighth, width), lambda i, o: (0, 0, which(i, o), 0)),
        ],
        pl.BlockSpec((1, rows, width), lambda i, o: (i, 0, 0)),
        (weights, twiddles),
        order,
        nbytes=16 * rows * width,
    )


def pair_kernel(order, near, far, *rest):
    outs = rest[-3:]
    for i, out in enumerate(outs):
        out[0] = near[i + 1]
        out[1] = far[i + 1]


def pair_up(order, near, far, after):
    _, rows, width = near.shape
    whole = pl.BlockSpec((4, rows, width), lambda i, o: (0, 0, 0))
    return call(
        pair_kernel,
        [jax.ShapeDtypeStruct((2, rows, width), near.dtype)] * 3,
        (1,),
        [whole, whole, *[pl.BlockSpec(memory_space=pl.ANY)] * len(after)],
        [pl.BlockSpec((2, rows, width), lambda i, o: (0, 0, 0))] * 3,
        (near, far, *after),
        order,
        nbytes=24 * rows * width,
    )


def gathered_kernel(laws, order, near, far, one, two, three, maps, *rest):
    *_, out_0, out_1, out_2, out_3, both = rest
    width = maps.shape[-1]
    outs = (out_0, out_1, out_2, out_3)
    slots = near.shape[1] // (laws + 2)
    for index, bit in enumerate((FIRST, SECOND, THIRD)):
        child = lax.div(order[0], bit) & 1
        for source in range(2):
            for goal in range(2):
                part = maps[index, child ^ goal, child ^ source]
                turned = roll_half(part.astype(jnp.float32)).astype(part.dtype)
                at = slice(source * width, (source + 1) * width)
                both[index, at, goal * width : (goal + 1) * width] = part
                both[index, at, (2 + goal) * width : (3 + goal) * width] = turned

    def piece(place, start, size):
        at = pl.ds(pl.multiple_of(start, 16), size)
        plane = PLANE.index(place & (FIRST | THIRD))
        if plane == 0:
            return (far if place & SECOND else near)[0, at, :]
        return (one, two, three)[plane - 1][1 if place & SECOND else 0, at, :]

    step_slots = 16

    def step(i, carry):
        rows = step_slots * laws
        values = [piece(place, i * rows, rows) for place in range(8)]
        for index, bit in enumerate((FIRST, SECOND, THIRD)):
            for place in range(8):
                if place & bit:
                    continue
                joint = jnp.concatenate([values[place], values[place | bit]], axis=1)
                state = jnp.dot(joint, both[index], preferred_element_type=jnp.float32)
                for goal in range(2):
                    mine = place | bit if goal else place
                    plain = state[:, goal * width : (goal + 1) * width]
                    if index < 2:
                        turned = state[:, (2 + goal) * width : (3 + goal) * width]
                        start = slots * laws + index * slots + i * step_slots
                        factors = piece(mine, start, step_slots).astype(jnp.float32)
                        values[mine] = twist(plain, turned, factors).astype(jnp.bfloat16)
                    else:
                        out = outs[PLANE.index(mine & (FIRST | THIRD))]
                        at = pl.ds(pl.multiple_of(i * rows, 16), rows)
                        out[1 if mine & SECOND else 0, at, :] = plain.astype(out.dtype)
        return carry

    lax.fori_loop(0, slots // step_slots, step, 0)


def gathered_levels(order, near, far, received, kernels, laws, after):
    _, rows, width = near.shape
    full = rows // (laws + 2) * laws
    first = pl.BlockSpec((1, rows, width), lambda i, o: (0, 0, 0))
    pair = pl.BlockSpec((2, rows, width), lambda i, o: (0, 0, 0))
    return call(
        functools.partial(gathered_kernel, laws),
        [jax.ShapeDtypeStruct((2, full, width), near.dtype)] * 4,
        (1,),
        [
            *(first, first, pair, pair, pair),
            pl.BlockSpec(kernels.shape, lambda i, o: (0, 0, 0, 0, 0)),
            *[pl.BlockSpec(memory_space=pl.ANY)] * len(after),
        ],
        [pl.BlockSpec((2, full, width), lambda i, o: (0, 0, 0))] * 4,
        (near, far, *received, kernels, *after),
        order,
        scratch=[pltpu.VMEM((3, 2 * width, 4 * width), near.dtype)],
        flops=3 * 8 * full * 4 * width * width,
        nbytes=32 * full * width,
    )


def far_kernel(order, a, b, c, d, out):
    for i, block in enumerate((a, b, c, d)):
        out[i] = block[0]


def far_part(order, blocks):
    _, rows, width = blocks[0].shape
    return call(
        far_kernel,
        jax.ShapeDtypeStruct((4, rows, width), blocks[0].dtype),
        (1,),
        [pl.BlockSpec((1, rows, width), lambda i, o: (1, 0, 0))] * 4,
        pl.BlockSpec((4, rows, width), lambda i, o: (0, 0, 0)),
        blocks,
        order,
        nbytes=16 * rows * width,
    )


def unpack_kernel(order, *refs):
    *blocks, t, _, out = refs
    targets, slots, laws, width = out.shape
    rows = slots * laws

    def write(block):
        for target in range(targets):
            state = block[0, target * rows : (target + 1) * rows, :]
            out[target] = twist_16(state, t[0, target]).astype(out.dtype).reshape(out.shape[1:])

    if len(blocks) == 1:
        write(blocks[0])
    else:
        for i, block in enumerate(blocks):
            pl.when(pl.program_id(0) == i)(functools.partial(write, block))


def unpack(order, blocks, twiddles, whole, far):
    _, slots, laws, width = whole.shape
    eighth = slots // 8
    rows = GATHERED * eighth * laws

    def which(i, o):
        return o[lax.div(i, 2) * FIRST + lax.rem(i, 2) * THIRD + far]

    if len(blocks) == 1:
        block_specs = [pl.BlockSpec((1, rows, width), lambda i, o: (i, 0, 0))]
    else:
        block_specs = [pl.BlockSpec((1, rows, width), lambda i, o: (0, 0, 0))] * 4
    return call(
        unpack_kernel,
        jax.ShapeDtypeStruct(whole.shape, whole.dtype),
        (4,),
        [
            *block_specs,
            pl.BlockSpec((1, GATHERED, eighth, width), lambda i, o: (3, 0, which(i, o), 0)),
            pl.BlockSpec(memory_space=pl.ANY),
        ],
        pl.BlockSpec((GATHERED, eighth, laws, width), lambda i, o: (0, which(i, o), 0, 0)),
        (*blocks, twiddles, whole),
        order,
        aliases={len(blocks) + 2: 0},
        nbytes=16 * rows * width,
    )


def body(weights_in, twiddles, kernels):
    targets, _, laws, _ = weights_in.shape
    order = my_order()
    far_send = pack(order, weights_in, twiddles, SECOND)
    far = swap(far_send, SECOND)
    near = pack(order, weights_in, twiddles, 0)
    swapped = list(range(GATHERED, targets))
    state = {}
    for target in swapped:
        own = first_twist(order, weights_in, twiddles, target, far_send)
        state[target] = own, swap(own, FIRST)
    for target in swapped:
        own = level(order, *state[target], kernels, twiddles, 0, FIRST, target)
        state[target] = own, swap(own, SECOND)
    pairs = pair_up(order, near, far, [state[target][0] for target in swapped])
    received = [swap(pair, place) for pair, place in zip(pairs, PLANE[1:])]
    for target in swapped:
        own = level(order, *state[target], kernels, twiddles, 1, SECOND, target)
        state[target] = own, swap(own, THIRD)
    done = gathered_levels(order, near, far, received, kernels, laws, [state[swapped[0]][0]])
    back = [done[0], *[swap(block, place) for block, place in zip(done[1:], PLANE[1:])]]
    far_back = swap(far_part(order, back), SECOND)
    whole = None
    for target in swapped:
        whole = level(order, *state[target], kernels, twiddles, 2, THIRD, target, whole, True)
    whole = unpack(order, back, twiddles, whole, 0)
    return unpack(order, [far_back], twiddles, whole, SECOND)


def solution(mesh):
    return jax.shard_map(
        body,
        mesh=mesh,
        in_specs=(P(None, ("src", "tgt"), None, None), P(None, None, ("src", "tgt"), None), P()),
        out_specs=P(None, ("src", "tgt"), None, None),
        check_vma=False,
    )
```

```python
import functools

import jax
import jax.numpy as jnp
from jax import lax
from jax.experimental import pallas as pl
from jax.experimental.pallas import tpu as pltpu
from jax.sharding import PartitionSpec as P

FIRST, SECOND, THIRD = 4, 2, 1
GATHERED = 2
PIECES = (2, 3, 3)
COST = 4
VMEM = 48 * 2**20


def swap(block, mask):
    n_src, n_tgt = lax.axis_size("src"), lax.axis_size("tgt")
    flip_src = (n_src // 2 if mask & FIRST else 0) + (n_src // 4 if mask & SECOND else 0)
    flip_tgt = n_tgt // 2 if mask & THIRD else 0
    if not flip_tgt:
        return lax.ppermute(block, "src", [(i, i ^ flip_src) for i in range(n_src)])
    if not flip_src:
        return lax.ppermute(block, "tgt", [(i, i ^ flip_tgt) for i in range(n_tgt)])
    route = []
    for i in range(n_src):
        for j in range(n_tgt):
            route.append((i * n_tgt + j, (i ^ flip_src) * n_tgt + (j ^ flip_tgt)))
    return lax.ppermute(block, ("src", "tgt"), route)


def my_order():
    n_src, n_tgt = lax.axis_size("src"), lax.axis_size("tgt")
    place = lax.axis_index("src") // (n_src // 4) * 2 + lax.axis_index("tgt") // (n_tgt // 2)
    return jnp.bitwise_xor(place.astype(jnp.int32), jnp.arange(8, dtype=jnp.int32))


def roll_half(block):
    return pltpu.roll(block, block.shape[-1] // 2, 1)


def phases(rows):
    turned = roll_half(rows)
    low = lax.broadcasted_iota(jnp.int32, rows.shape, 1) < rows.shape[-1] // 2
    return jnp.where(low, rows, turned)[:, None, :], jnp.where(low, -turned, rows)[:, None, :]


def twist(plain, turned, rows):
    co, si = phases(rows)
    shape = (rows.shape[0], plain.shape[0] // rows.shape[0], plain.shape[1])
    return (plain.reshape(shape) * co + turned.reshape(shape) * si).reshape(plain.shape)


def twist_16(block, rows):
    wide = block.astype(jnp.float32)
    return twist(wide, roll_half(wide), rows)


def call(kernel, out_shape, grid, in_specs, out_specs, args, order, scratch=(), aliases=None, flops=0, nbytes=0):
    return pl.pallas_call(
        kernel,
        out_shape=out_shape,
        grid_spec=pltpu.PrefetchScalarGridSpec(
            num_scalar_prefetch=1, grid=grid, in_specs=in_specs, out_specs=out_specs, scratch_shapes=list(scratch)
        ),
        input_output_aliases=aliases or {},
        compiler_params=pltpu.CompilerParams(vmem_limit_bytes=VMEM),
        cost_estimate=pl.CostEstimate(flops=COST * flops, bytes_accessed=COST * nbytes, transcendentals=0),
    )(order, *args)


def pieces(targets, slots):
    per_target = sum(PIECES) // (targets - GATHERED)
    starts = [GATHERED * per_target + sum(PIECES[:i]) for i in range(len(PIECES))]
    return [(start, count, per_target) for start, count in zip(starts, PIECES)]


def spot(i, piece):
    start, _, per_target = piece
    return lax.div(start + i, per_target), lax.rem(start + i, per_target)


def first_kernel(order, w, t, _, out):
    slots, laws, width = out.shape
    out[...] = twist_16(w[...].reshape(slots * laws, width), t[...]).astype(out.dtype).reshape(out.shape)


def first_twist(order, weights, twiddles, piece, after):
    _, slots, laws, width = weights.shape
    tile, tiles = slots // piece[2], piece[1]
    return call(
        first_kernel,
        jax.ShapeDtypeStruct((tiles * tile, laws, width), weights.dtype),
        (tiles,),
        [
            pl.BlockSpec((None, tile, laws, width), lambda i, o: (*spot(i, piece), 0, 0)),
            pl.BlockSpec((None, None, tile, width), lambda i, o: (0, *spot(i, piece), 0)),
            pl.BlockSpec(memory_space=pl.ANY),
        ],
        pl.BlockSpec((tile, laws, width), lambda i, o: (i, 0, 0)),
        (weights, twiddles, after),
        order,
        nbytes=4 * tiles * tile * laws * width,
    )


def level_kernel(bit, order, own, other, maps, t, *rest):
    out, both = rest[-2:]
    slots, laws, width = own.shape

    @pl.when(pl.program_id(0) == 0)
    def _():
        child = lax.div(order[0], bit) & 1
        for source in range(2):
            part = maps[child, child if source == 0 else 1 - child]
            both[source * width : (source + 1) * width, :width] = part
            turned = roll_half(part.astype(jnp.float32)).astype(part.dtype)
            both[source * width : (source + 1) * width, width:] = turned

    rows = slots * laws
    state = jnp.dot(own[...].reshape(rows, width), both[:width, :], preferred_element_type=jnp.float32)
    state += jnp.dot(other[...].reshape(rows, width), both[width:, :], preferred_element_type=jnp.float32)
    out[...] = twist(state[:, :width], state[:, width:], t[...]).astype(out.dtype).reshape(out.shape)


def level(order, own, other, kernels, twiddles, index, bit, piece, whole=None):
    slots, laws, width = own.shape
    tiles = piece[1]
    tile = slots // tiles
    block = pl.BlockSpec((tile, laws, width), lambda i, o: (i, 0, 0))
    in_specs = [
        block,
        block,
        pl.BlockSpec((None, 2, 2, width, width), lambda i, o: (index, 0, 0, 0, 0)),
        pl.BlockSpec((None, None, tile, width), lambda i, o: (index + 1, *spot(i, piece), 0)),
    ]
    args, aliases = [own, other, kernels, twiddles], {}
    out_shape, out_spec = jax.ShapeDtypeStruct(own.shape, own.dtype), block
    if index == 2:
        out_shape = jax.ShapeDtypeStruct((*twiddles.shape[1:3], laws, width), own.dtype)
        out_spec = pl.BlockSpec((None, tile, laws, width), lambda i, o: (*spot(i, piece), 0, 0))
    if whole is not None:
        args.append(whole)
        in_specs.append(pl.BlockSpec(memory_space=pl.ANY))
        aliases = {5: 0}
    return call(
        functools.partial(level_kernel, bit),
        out_shape,
        (tiles,),
        in_specs,
        out_spec,
        args,
        order,
        scratch=[pltpu.VMEM((2 * width, 2 * width), own.dtype)],
        aliases=aliases,
        flops=8 * slots * laws * width * width,
        nbytes=6 * slots * laws * width,
    )


PLANE = (0, THIRD, FIRST, FIRST | THIRD)


def pack_kernel(order, w, t, out):
    targets, slots, laws, width = w.shape
    rows = slots * laws
    for target in range(targets):
        block = twist_16(w[target].reshape(rows, width), t[0, target])
        out[0, target * rows : (target + 1) * rows, :] = block.astype(out.dtype)
        for later in range(2):
            start = targets * rows + (later * targets + target) * slots
            out[0, start : start + slots, :] = t[1 + later, target].astype(out.dtype)


def pack(order, weights, twiddles, far):
    _, slots, laws, width = weights.shape
    eighth = slots // 8
    rows = GATHERED * eighth * (laws + 2)

    def which(i, o):
        return o[lax.div(i, 2) * FIRST + lax.rem(i, 2) * THIRD + far]

    return call(
        pack_kernel,
        jax.ShapeDtypeStruct((4, rows, width), weights.dtype),
        (4,),
        [
            pl.BlockSpec((GATHERED, eighth, laws, width), lambda i, o: (0, which(i, o), 0, 0)),
            pl.BlockSpec((3, GATHERED, eighth, width), lambda i, o: (0, 0, which(i, o), 0)),
        ],
        pl.BlockSpec((1, rows, width), lambda i, o: (i, 0, 0)),
        (weights, twiddles),
        order,
        nbytes=16 * rows * width,
    )


def pair_kernel(order, near, far, *rest):
    outs = rest[-3:]
    for i, out in enumerate(outs):
        out[0] = near[i + 1]
        out[1] = far[i + 1]


def pair_up(order, near, far, after):
    _, rows, width = near.shape
    whole = pl.BlockSpec((4, rows, width), lambda i, o: (0, 0, 0))
    return call(
        pair_kernel,
        [jax.ShapeDtypeStruct((2, rows, width), near.dtype)] * 3,
        (1,),
        [whole, whole, *[pl.BlockSpec(memory_space=pl.ANY)] * len(after)],
        [pl.BlockSpec((2, rows, width), lambda i, o: (0, 0, 0))] * 3,
        (near, far, *after),
        order,
        nbytes=24 * rows * width,
    )


def gathered_kernel(laws, order, near, far, one, two, three, maps, *rest):
    *_, out_0, out_1, out_2, out_3, both = rest
    width = maps.shape[-1]
    outs = (out_0, out_1, out_2, out_3)
    slots = near.shape[1] // (laws + 2)
    for index, bit in enumerate((FIRST, SECOND, THIRD)):
        child = lax.div(order[0], bit) & 1
        for source in range(2):
            for goal in range(2):
                part = maps[index, child ^ goal, child ^ source]
                turned = roll_half(part.astype(jnp.float32)).astype(part.dtype)
                at = slice(source * width, (source + 1) * width)
                both[index, at, goal * width : (goal + 1) * width] = part
                both[index, at, (2 + goal) * width : (3 + goal) * width] = turned

    def piece(place, start, size):
        at = pl.ds(pl.multiple_of(start, 16), size)
        plane = PLANE.index(place & (FIRST | THIRD))
        if plane == 0:
            return (far if place & SECOND else near)[0, at, :]
        return (one, two, three)[plane - 1][1 if place & SECOND else 0, at, :]

    step_slots = 16

    def step(i, carry):
        rows = step_slots * laws
        values = [piece(place, i * rows, rows) for place in range(8)]
        for index, bit in enumerate((FIRST, SECOND, THIRD)):
            for place in range(8):
                if place & bit:
                    continue
                joint = jnp.concatenate([values[place], values[place | bit]], axis=1)
                state = jnp.dot(joint, both[index], preferred_element_type=jnp.float32)
                for goal in range(2):
                    mine = place | bit if goal else place
                    plain = state[:, goal * width : (goal + 1) * width]
                    if index < 2:
                        turned = state[:, (2 + goal) * width : (3 + goal) * width]
                        start = slots * laws + index * slots + i * step_slots
                        factors = piece(mine, start, step_slots).astype(jnp.float32)
                        values[mine] = twist(plain, turned, factors).astype(jnp.bfloat16)
                    else:
                        out = outs[PLANE.index(mine & (FIRST | THIRD))]
                        at = pl.ds(pl.multiple_of(i * rows, 16), rows)
                        out[1 if mine & SECOND else 0, at, :] = plain.astype(out.dtype)
        return carry

    lax.fori_loop(0, slots // step_slots, step, 0)


def gathered_levels(order, near, far, received, kernels, laws, after):
    _, rows, width = near.shape
    full = rows // (laws + 2) * laws
    first = pl.BlockSpec((1, rows, width), lambda i, o: (0, 0, 0))
    pair = pl.BlockSpec((2, rows, width), lambda i, o: (0, 0, 0))
    return call(
        functools.partial(gathered_kernel, laws),
        [jax.ShapeDtypeStruct((2, full, width), near.dtype)] * 4,
        (1,),
        [
            *(first, first, pair, pair, pair),
            pl.BlockSpec(kernels.shape, lambda i, o: (0, 0, 0, 0, 0)),
            *[pl.BlockSpec(memory_space=pl.ANY)] * len(after),
        ],
        [pl.BlockSpec((2, full, width), lambda i, o: (0, 0, 0))] * 4,
        (near, far, *received, kernels, *after),
        order,
        scratch=[pltpu.VMEM((3, 2 * width, 4 * width), near.dtype)],
        flops=3 * 8 * full * 4 * width * width,
        nbytes=32 * full * width,
    )


def far_kernel(order, a, b, c, d, *rest):
    out = rest[-1]
    for i, block in enumerate((a, b, c, d)):
        out[i] = block[0]


def far_part(order, blocks, after):
    _, rows, width = blocks[0].shape
    return call(
        far_kernel,
        jax.ShapeDtypeStruct((4, rows, width), blocks[0].dtype),
        (1,),
        [*[pl.BlockSpec((1, rows, width), lambda i, o: (1, 0, 0))] * 4, *[pl.BlockSpec(memory_space=pl.ANY)] * len(after)],
        pl.BlockSpec((4, rows, width), lambda i, o: (0, 0, 0)),
        (*blocks, *after),
        order,
        nbytes=16 * rows * width,
    )


def unpack_kernel(order, *refs):
    *blocks, t, _, out = refs
    targets, slots, laws, width = out.shape
    rows = slots * laws

    def write(block):
        for target in range(targets):
            state = block[0, target * rows : (target + 1) * rows, :]
            out[target] = twist_16(state, t[0, target]).astype(out.dtype).reshape(out.shape[1:])

    if len(blocks) == 1:
        write(blocks[0])
    else:
        for i, block in enumerate(blocks):
            pl.when(pl.program_id(0) == i)(functools.partial(write, block))


def unpack(order, blocks, twiddles, whole, far):
    _, slots, laws, width = whole.shape
    eighth = slots // 8
    rows = GATHERED * eighth * laws

    def which(i, o):
        return o[lax.div(i, 2) * FIRST + lax.rem(i, 2) * THIRD + far]

    if len(blocks) == 1:
        block_specs = [pl.BlockSpec((1, rows, width), lambda i, o: (i, 0, 0))]
    else:
        block_specs = [pl.BlockSpec((1, rows, width), lambda i, o: (0, 0, 0))] * 4
    return call(
        unpack_kernel,
        jax.ShapeDtypeStruct(whole.shape, whole.dtype),
        (4,),
        [
            *block_specs,
            pl.BlockSpec((1, GATHERED, eighth, width), lambda i, o: (3, 0, which(i, o), 0)),
            pl.BlockSpec(memory_space=pl.ANY),
        ],
        pl.BlockSpec((GATHERED, eighth, laws, width), lambda i, o: (0, which(i, o), 0, 0)),
        (*blocks, twiddles, whole),
        order,
        aliases={len(blocks) + 2: 0},
        nbytes=16 * rows * width,
    )


def body(weights_in, twiddles, kernels):
    targets, slots, laws, _ = weights_in.shape
    order = my_order()
    far_send = pack(order, weights_in, twiddles, SECOND)
    far = swap(far_send, SECOND)
    near = pack(order, weights_in, twiddles, 0)
    cuts = pieces(targets, slots)
    own = [first_twist(order, weights_in, twiddles, piece, far_send) for piece in cuts]

    def next_level(index, bit, own, other):
        return [level(order, *pair, kernels, twiddles, index, bit, piece) for *pair, piece in zip(own, other, cuts)]

    own = next_level(0, FIRST, own, [swap(block, FIRST) for block in own])
    pairs = pair_up(order, near, far, own)
    received = [swap(pair, place) for pair, place in zip(pairs, PLANE[1:])]
    own = next_level(1, SECOND, own, [swap(block, SECOND) for block in own])
    other = [swap(block, THIRD) for block in own]
    whole = level(order, own[0], other[0], kernels, twiddles, 2, THIRD, cuts[0])
    done = gathered_levels(order, near, far, received, kernels, laws, own[:1])
    back = [done[0], *[swap(block, place) for block, place in zip(done[1:], PLANE[1:])]]
    far_back = swap(far_part(order, back, [own[-2], whole]), SECOND)
    for *pair, piece in list(zip(own, other, cuts))[1:]:
        whole = level(order, *pair, kernels, twiddles, 2, THIRD, piece, whole)
    whole = unpack(order, back, twiddles, whole, 0)
    return unpack(order, [far_back], twiddles, whole, SECOND)


def solution(mesh):
    return jax.shard_map(
        body,
        mesh=mesh,
        in_specs=(P(None, ("src", "tgt"), None, None), P(None, None, ("src", "tgt"), None), P()),
        out_specs=P(None, ("src", "tgt"), None, None),
        check_vma=False,
    )
```

```python
import functools

import jax
import jax.numpy as jnp
from jax import lax
from jax.experimental import pallas as pl
from jax.experimental.pallas import tpu as pltpu
from jax.sharding import PartitionSpec as P

FIRST, SECOND, THIRD = 4, 2, 1
GATHERED = 2
PIECES = (2, 3, 3)
FIRST_ORDER = (0, 1, 2)
LEVEL_ORDER = (0, 1, 2)
COST = 4
TCOST = 0
LCOST = 12
NCOST = 4
VMEM = 48 * 2**20


def swap(block, mask):
    n_src, n_tgt = lax.axis_size("src"), lax.axis_size("tgt")
    flip_src = (n_src // 2 if mask & FIRST else 0) + (n_src // 4 if mask & SECOND else 0)
    flip_tgt = n_tgt // 2 if mask & THIRD else 0
    if not flip_tgt:
        return lax.ppermute(block, "src", [(i, i ^ flip_src) for i in range(n_src)])
    if not flip_src:
        return lax.ppermute(block, "tgt", [(i, i ^ flip_tgt) for i in range(n_tgt)])
    route = []
    for i in range(n_src):
        for j in range(n_tgt):
            route.append((i * n_tgt + j, (i ^ flip_src) * n_tgt + (j ^ flip_tgt)))
    return lax.ppermute(block, ("src", "tgt"), route)


def my_order():
    n_src, n_tgt = lax.axis_size("src"), lax.axis_size("tgt")
    place = lax.axis_index("src") // (n_src // 4) * 2 + lax.axis_index("tgt") // (n_tgt // 2)
    return jnp.bitwise_xor(place.astype(jnp.int32), jnp.arange(8, dtype=jnp.int32))


def roll_half(block):
    return pltpu.roll(block, block.shape[-1] // 2, 1)


def phases(rows):
    turned = roll_half(rows)
    low = lax.broadcasted_iota(jnp.int32, rows.shape, 1) < rows.shape[-1] // 2
    return jnp.where(low, rows, turned)[:, None, :], jnp.where(low, -turned, rows)[:, None, :]


def twist(plain, turned, rows):
    co, si = phases(rows)
    shape = (rows.shape[0], plain.shape[0] // rows.shape[0], plain.shape[1])
    return (plain.reshape(shape) * co + turned.reshape(shape) * si).reshape(plain.shape)


def twist_16(block, rows):
    width = block.shape[-1]
    row = lax.broadcasted_iota(jnp.int32, (width, width), 0)
    column = lax.broadcasted_iota(jnp.int32, (width, width), 1)
    exchange = (jnp.abs(row - column) == width // 2).astype(jnp.float32).astype(block.dtype)
    turned = jnp.dot(block, exchange, preferred_element_type=jnp.float32)
    return twist(block.astype(jnp.float32), turned, rows)


def call(kernel, out_shape, grid, in_specs, out_specs, args, order, scratch=(), aliases=None, cost=COST, flops=0, nbytes=0):
    return pl.pallas_call(
        kernel,
        out_shape=out_shape,
        grid_spec=pltpu.PrefetchScalarGridSpec(
            num_scalar_prefetch=1, grid=grid, in_specs=in_specs, out_specs=out_specs, scratch_shapes=list(scratch)
        ),
        input_output_aliases=aliases or {},
        compiler_params=pltpu.CompilerParams(vmem_limit_bytes=VMEM),
        cost_estimate=pl.CostEstimate(flops=cost * flops, bytes_accessed=cost * nbytes, transcendentals=0),
    )(order, *args)


def pieces(targets, slots):
    per_target = sum(PIECES) // (targets - GATHERED)
    starts = [GATHERED * per_target + sum(PIECES[:i]) for i in range(len(PIECES))]
    return [(start, count, per_target) for start, count in zip(starts, PIECES)]


def spot(i, piece):
    start, _, per_target = piece
    return lax.div(start + i, per_target), lax.rem(start + i, per_target)


def first_kernel(order, w, t, _, out):
    slots, laws, width = out.shape
    out[...] = twist_16(w[...].reshape(slots * laws, width), t[...]).astype(out.dtype).reshape(out.shape)


def first_twist(order, weights, twiddles, piece, after):
    _, slots, laws, width = weights.shape
    tile, tiles = slots // piece[2], piece[1]
    return call(
        first_kernel,
        jax.ShapeDtypeStruct((tiles * tile, laws, width), weights.dtype),
        (tiles,),
        [
            pl.BlockSpec((None, tile, laws, width), lambda i, o: (*spot(i, piece), 0, 0)),
            pl.BlockSpec((None, None, tile, width), lambda i, o: (0, *spot(i, piece), 0)),
            pl.BlockSpec(memory_space=pl.ANY),
        ],
        pl.BlockSpec((tile, laws, width), lambda i, o: (i, 0, 0)),
        (weights, twiddles, after),
        order,
        cost=TCOST,
        nbytes=4 * tiles * tile * laws * width,
    )


def level_kernel(bit, order, own, other, maps, t, *rest):
    out, both = rest[-2:]
    slots, laws, width = own.shape

    @pl.when(pl.program_id(0) == 0)
    def _():
        child = lax.div(order[0], bit) & 1
        for source in range(2):
            part = maps[child, child if source == 0 else 1 - child]
            both[source * width : (source + 1) * width, :width] = part
            turned = roll_half(part.astype(jnp.float32)).astype(part.dtype)
            both[source * width : (source + 1) * width, width:] = turned

    rows = slots * laws
    state = jnp.dot(own[...].reshape(rows, width), both[:width, :], preferred_element_type=jnp.float32)
    state += jnp.dot(other[...].reshape(rows, width), both[width:, :], preferred_element_type=jnp.float32)
    out[...] = twist(state[:, :width], state[:, width:], t[...]).astype(out.dtype).reshape(out.shape)


def level(order, own, other, kernels, twiddles, index, bit, piece, whole=None, after=()):
    slots, laws, width = own.shape
    tiles = piece[1]
    tile = slots // tiles
    block = pl.BlockSpec((tile, laws, width), lambda i, o: (i, 0, 0))
    in_specs = [
        block,
        block,
        pl.BlockSpec((None, 2, 2, width, width), lambda i, o: (index, 0, 0, 0, 0)),
        pl.BlockSpec((None, None, tile, width), lambda i, o: (index + 1, *spot(i, piece), 0)),
    ]
    args, aliases = [own, other, kernels, twiddles], {}
    out_shape, out_spec = jax.ShapeDtypeStruct(own.shape, own.dtype), block
    if index == 2:
        out_shape = jax.ShapeDtypeStruct((*twiddles.shape[1:3], laws, width), own.dtype)
        out_spec = pl.BlockSpec((None, tile, laws, width), lambda i, o: (*spot(i, piece), 0, 0))
    if whole is not None:
        args.append(whole)
        in_specs.append(pl.BlockSpec(memory_space=pl.ANY))
        aliases = {5: 0}
    args += after
    in_specs += [pl.BlockSpec(memory_space=pl.ANY)] * len(after)
    return call(
        functools.partial(level_kernel, bit),
        out_shape,
        (tiles,),
        in_specs,
        out_spec,
        args,
        order,
        scratch=[pltpu.VMEM((2 * width, 2 * width), own.dtype)],
        aliases=aliases,
        cost=COST if index else (LCOST if piece[1] == PIECES[0] else 0),
        flops=8 * slots * laws * width * width,
        nbytes=6 * slots * laws * width,
    )


PLANE = (0, THIRD, FIRST, FIRST | THIRD)


def pack_kernel(order, w, t, *rest):
    out = rest[-1]
    targets, slots, laws, width = w.shape
    rows = slots * laws
    for target in range(targets):
        block = twist_16(w[target].reshape(rows, width), t[0, target])
        out[0, target * rows : (target + 1) * rows, :] = block.astype(out.dtype)
        for later in range(2):
            start = targets * rows + (later * targets + target) * slots
            out[0, start : start + slots, :] = t[1 + later, target].astype(out.dtype)


def pack(order, weights, twiddles, far, after=()):
    _, slots, laws, width = weights.shape
    eighth = slots // 8
    rows = GATHERED * eighth * (laws + 2)

    def which(i, o):
        return o[lax.div(i, 2) * FIRST + lax.rem(i, 2) * THIRD + far]

    return call(
        pack_kernel,
        jax.ShapeDtypeStruct((4, rows, width), weights.dtype),
        (4,),
        [
            pl.BlockSpec((GATHERED, eighth, laws, width), lambda i, o: (0, which(i, o), 0, 0)),
            pl.BlockSpec((3, GATHERED, eighth, width), lambda i, o: (0, 0, which(i, o), 0)),
            *[pl.BlockSpec(memory_space=pl.ANY)] * len(after),
        ],
        pl.BlockSpec((1, rows, width), lambda i, o: (i, 0, 0)),
        (weights, twiddles, *after),
        order,
        cost=NCOST,
        nbytes=16 * rows * width,
    )


def pair_kernel(order, near, far, *rest):
    outs = rest[-3:]
    for i, out in enumerate(outs):
        out[0] = near[i + 1]
        out[1] = far[i + 1]


def pair_up(order, near, far, after):
    _, rows, width = near.shape
    whole = pl.BlockSpec((4, rows, width), lambda i, o: (0, 0, 0))
    return call(
        pair_kernel,
        [jax.ShapeDtypeStruct((2, rows, width), near.dtype)] * 3,
        (1,),
        [whole, whole, *[pl.BlockSpec(memory_space=pl.ANY)] * len(after)],
        [pl.BlockSpec((2, rows, width), lambda i, o: (0, 0, 0))] * 3,
        (near, far, *after),
        order,
        nbytes=24 * rows * width,
    )


def gathered_kernel(laws, order, near, far, one, two, three, maps, *rest):
    *_, out_0, out_1, out_2, out_3, both = rest
    width = maps.shape[-1]
    outs = (out_0, out_1, out_2, out_3)
    slots = near.shape[1] // (laws + 2)
    for index, bit in enumerate((FIRST, SECOND, THIRD)):
        child = lax.div(order[0], bit) & 1
        for source in range(2):
            for goal in range(2):
                part = maps[index, child ^ goal, child ^ source]
                turned = roll_half(part.astype(jnp.float32)).astype(part.dtype)
                at = slice(source * width, (source + 1) * width)
                both[index, at, goal * width : (goal + 1) * width] = part
                both[index, at, (2 + goal) * width : (3 + goal) * width] = turned

    def piece(place, start, size):
        at = pl.ds(pl.multiple_of(start, 16), size)
        plane = PLANE.index(place & (FIRST | THIRD))
        if plane == 0:
            return (far if place & SECOND else near)[0, at, :]
        return (one, two, three)[plane - 1][1 if place & SECOND else 0, at, :]

    step_slots = 16

    def step(i, carry):
        rows = step_slots * laws
        values = [piece(place, i * rows, rows) for place in range(8)]
        for index, bit in enumerate((FIRST, SECOND, THIRD)):
            for place in range(8):
                if place & bit:
                    continue
                joint = jnp.concatenate([values[place], values[place | bit]], axis=1)
                state = jnp.dot(joint, both[index], preferred_element_type=jnp.float32)
                for goal in range(2):
                    mine = place | bit if goal else place
                    plain = state[:, goal * width : (goal + 1) * width]
                    if index < 2:
                        turned = state[:, (2 + goal) * width : (3 + goal) * width]
                        start = slots * laws + index * slots + i * step_slots
                        factors = piece(mine, start, step_slots).astype(jnp.float32)
                        values[mine] = twist(plain, turned, factors).astype(jnp.bfloat16)
                    else:
                        out = outs[PLANE.index(mine & (FIRST | THIRD))]
                        at = pl.ds(pl.multiple_of(i * rows, 16), rows)
                        out[1 if mine & SECOND else 0, at, :] = plain.astype(out.dtype)
        return carry

    lax.fori_loop(0, slots // step_slots, step, 0)


def gathered_levels(order, near, far, received, kernels, laws, after):
    _, rows, width = near.shape
    full = rows // (laws + 2) * laws
    first = pl.BlockSpec((1, rows, width), lambda i, o: (0, 0, 0))
    pair = pl.BlockSpec((2, rows, width), lambda i, o: (0, 0, 0))
    return call(
        functools.partial(gathered_kernel, laws),
        [jax.ShapeDtypeStruct((2, full, width), near.dtype)] * 4,
        (1,),
        [
            *(first, first, pair, pair, pair),
            pl.BlockSpec(kernels.shape, lambda i, o: (0, 0, 0, 0, 0)),
            *[pl.BlockSpec(memory_space=pl.ANY)] * len(after),
        ],
        [pl.BlockSpec((2, full, width), lambda i, o: (0, 0, 0))] * 4,
        (near, far, *received, kernels, *after),
        order,
        scratch=[pltpu.VMEM((3, 2 * width, 4 * width), near.dtype)],
        flops=3 * 8 * full * 4 * width * width,
        nbytes=32 * full * width,
    )


def far_kernel(order, a, b, c, d, *rest):
    out = rest[-1]
    for i, block in enumerate((a, b, c, d)):
        out[i] = block[0]


def far_part(order, blocks, after):
    _, rows, width = blocks[0].shape
    return call(
        far_kernel,
        jax.ShapeDtypeStruct((4, rows, width), blocks[0].dtype),
        (1,),
        [*[pl.BlockSpec((1, rows, width), lambda i, o: (1, 0, 0))] * 4, *[pl.BlockSpec(memory_space=pl.ANY)] * len(after)],
        pl.BlockSpec((4, rows, width), lambda i, o: (0, 0, 0)),
        (*blocks, *after),
        order,
        nbytes=16 * rows * width,
    )


def unpack_kernel(order, *refs):
    *blocks, t, _, out = refs
    targets, slots, laws, width = out.shape
    rows = slots * laws

    def write(block):
        for target in range(targets):
            state = block[0, target * rows : (target + 1) * rows, :]
            out[target] = twist_16(state, t[0, target]).astype(out.dtype).reshape(out.shape[1:])

    if len(blocks) == 1:
        write(blocks[0])
    else:
        for i, block in enumerate(blocks):
            pl.when(pl.program_id(0) == i)(functools.partial(write, block))


def unpack(order, blocks, twiddles, whole, far):
    _, slots, laws, width = whole.shape
    eighth = slots // 8
    rows = GATHERED * eighth * laws

    def which(i, o):
        return o[lax.div(i, 2) * FIRST + lax.rem(i, 2) * THIRD + far]

    if len(blocks) == 1:
        block_specs = [pl.BlockSpec((1, rows, width), lambda i, o: (i, 0, 0))]
    else:
        block_specs = [pl.BlockSpec((1, rows, width), lambda i, o: (0, 0, 0))] * 4
    return call(
        unpack_kernel,
        jax.ShapeDtypeStruct(whole.shape, whole.dtype),
        (4,),
        [
            *block_specs,
            pl.BlockSpec((1, GATHERED, eighth, width), lambda i, o: (3, 0, which(i, o), 0)),
            pl.BlockSpec(memory_space=pl.ANY),
        ],
        pl.BlockSpec((GATHERED, eighth, laws, width), lambda i, o: (0, which(i, o), 0, 0)),
        (*blocks, twiddles, whole),
        order,
        aliases={len(blocks) + 2: 0},
        nbytes=16 * rows * width,
    )


def body(weights_in, twiddles, kernels):
    targets, slots, laws, _ = weights_in.shape
    order = my_order()
    far_send = pack(order, weights_in, twiddles, SECOND)
    far = swap(far_send, SECOND)
    near = pack(order, weights_in, twiddles, 0, [far_send])
    cuts = pieces(targets, slots)
    own, after = [None] * len(cuts), far_send
    for i in FIRST_ORDER:
        own[i] = after = first_twist(order, weights_in, twiddles, cuts[i], after)
    other = [swap(block, FIRST) for block in own]
    first, after = [None] * len(cuts), []
    for i in LEVEL_ORDER:
        first[i] = level(order, own[i], other[i], kernels, twiddles, 0, FIRST, cuts[i], None, after)
        after = [first[i]]
    own = first

    def next_level(index, bit, own, other):
        return [level(order, *pair, kernels, twiddles, index, bit, piece) for *pair, piece in zip(own, other, cuts)]

    pairs = pair_up(order, near, far, own)
    received = [swap(pair, place) for pair, place in zip(pairs, PLANE[1:])]
    own = next_level(1, SECOND, own, [swap(block, SECOND) for block in own])
    other = [swap(block, THIRD) for block in own]
    whole = level(order, own[0], other[0], kernels, twiddles, 2, THIRD, cuts[0])
    done = gathered_levels(order, near, far, received, kernels, laws, own[:1])
    back = [done[0], *[swap(block, place) for block, place in zip(done[1:], PLANE[1:])]]
    far_back = swap(far_part(order, back, [own[-2], whole]), SECOND)
    for *pair, piece in list(zip(own, other, cuts))[1:]:
        whole = level(order, *pair, kernels, twiddles, 2, THIRD, piece, whole)
    whole = unpack(order, back, twiddles, whole, 0)
    return unpack(order, [far_back], twiddles, whole, SECOND)


def solution(mesh):
    return jax.shard_map(
        body,
        mesh=mesh,
        in_specs=(P(None, ("src", "tgt"), None, None), P(None, None, ("src", "tgt"), None), P()),
        out_specs=P(None, ("src", "tgt"), None, None),
        check_vma=False,
    )
```

```python
import functools

import jax
import jax.numpy as jnp
from jax import lax
from jax.experimental import pallas as pl
from jax.experimental.pallas import tpu as pltpu
from jax.sharding import PartitionSpec as P

FIRST, SECOND, THIRD = 4, 2, 1
GATHERED = 2
PIECES = (2, 3, 3)
FIRST_ORDER = (0, 1, 2)
LEVEL_ORDER = (0, 1, 2)
COST = 4
TCOST = 0
LCOST = 12
NCOST = 4
VMEM = 48 * 2**20


def swap(block, mask):
    n_src, n_tgt = lax.axis_size("src"), lax.axis_size("tgt")
    flip_src = (n_src // 2 if mask & FIRST else 0) + (n_src // 4 if mask & SECOND else 0)
    flip_tgt = n_tgt // 2 if mask & THIRD else 0
    if not flip_tgt:
        return lax.ppermute(block, "src", [(i, i ^ flip_src) for i in range(n_src)])
    if not flip_src:
        return lax.ppermute(block, "tgt", [(i, i ^ flip_tgt) for i in range(n_tgt)])
    route = []
    for i in range(n_src):
        for j in range(n_tgt):
            route.append((i * n_tgt + j, (i ^ flip_src) * n_tgt + (j ^ flip_tgt)))
    return lax.ppermute(block, ("src", "tgt"), route)


def my_place():
    n_src, n_tgt = lax.axis_size("src"), lax.axis_size("tgt")
    return lax.div(lax.axis_index("src"), n_src // 4) * 2 + lax.div(lax.axis_index("tgt"), n_tgt // 2)


def my_order():
    return jnp.bitwise_xor(my_place().astype(jnp.int32), jnp.arange(8, dtype=jnp.int32))


def roll_half(block):
    return pltpu.roll(block, block.shape[-1] // 2, 1)


def phases(rows):
    turned = roll_half(rows)
    low = lax.broadcasted_iota(jnp.int32, rows.shape, 1) < rows.shape[-1] // 2
    return jnp.where(low, rows, turned)[:, None, :], jnp.where(low, -turned, rows)[:, None, :]


def twist(plain, turned, rows):
    co, si = phases(rows)
    shape = (rows.shape[0], plain.shape[0] // rows.shape[0], plain.shape[1])
    return (plain.reshape(shape) * co + turned.reshape(shape) * si).reshape(plain.shape)


def twist_16(block, rows):
    width = block.shape[-1]
    row = lax.broadcasted_iota(jnp.int32, (width, width), 0)
    column = lax.broadcasted_iota(jnp.int32, (width, width), 1)
    exchange = (jnp.abs(row - column) == width // 2).astype(jnp.float32).astype(block.dtype)
    turned = jnp.dot(block, exchange, preferred_element_type=jnp.float32)
    return twist(block.astype(jnp.float32), turned, rows)


def call(kernel, out_shape, grid, in_specs, out_specs, args, order, scratch=(), aliases=None, vmem=VMEM, cost=COST, flops=0, nbytes=0):
    known = () if order is None else (order,)
    return pl.pallas_call(
        kernel,
        out_shape=out_shape,
        grid_spec=pltpu.PrefetchScalarGridSpec(
            num_scalar_prefetch=len(known), grid=grid, in_specs=in_specs, out_specs=out_specs, scratch_shapes=list(scratch)
        ),
        input_output_aliases=aliases or {},
        compiler_params=pltpu.CompilerParams(vmem_limit_bytes=vmem),
        cost_estimate=pl.CostEstimate(flops=cost * flops, bytes_accessed=cost * nbytes, transcendentals=0),
    )(*known, *args)


def pieces(targets, slots):
    per_target = sum(PIECES) // (targets - GATHERED)
    starts = [GATHERED * per_target + sum(PIECES[:i]) for i in range(len(PIECES))]
    return [(start, count, per_target) for start, count in zip(starts, PIECES)]


def spot(i, piece):
    start, _, per_target = piece
    return lax.div(start + i, per_target), lax.rem(start + i, per_target)


def first_kernel(order, w, t, _, out):
    slots, laws, width = out.shape
    out[...] = twist_16(w[...].reshape(slots * laws, width), t[...]).astype(out.dtype).reshape(out.shape)


def first_twist(order, weights, twiddles, piece, after):
    _, slots, laws, width = weights.shape
    tile, tiles = slots // piece[2], piece[1]
    return call(
        first_kernel,
        jax.ShapeDtypeStruct((tiles * tile, laws, width), weights.dtype),
        (tiles,),
        [
            pl.BlockSpec((None, tile, laws, width), lambda i, o: (*spot(i, piece), 0, 0)),
            pl.BlockSpec((None, None, tile, width), lambda i, o: (0, *spot(i, piece), 0)),
            pl.BlockSpec(memory_space=pl.ANY),
        ],
        pl.BlockSpec((tile, laws, width), lambda i, o: (i, 0, 0)),
        (weights, twiddles, after),
        order,
        cost=TCOST,
        nbytes=4 * tiles * tile * laws * width,
    )


def level_kernel(bit, order, own, other, maps, t, *rest):
    out, both = rest[-2:]
    slots, laws, width = own.shape

    @pl.when(pl.program_id(0) == 0)
    def _():
        child = lax.div(order[0], bit) & 1
        for source in range(2):
            part = maps[child, child if source == 0 else 1 - child]
            both[source * width : (source + 1) * width, :width] = part
            turned = roll_half(part.astype(jnp.float32)).astype(part.dtype)
            both[source * width : (source + 1) * width, width:] = turned

    rows = slots * laws
    state = jnp.dot(own[...].reshape(rows, width), both[:width, :], preferred_element_type=jnp.float32)
    state += jnp.dot(other[...].reshape(rows, width), both[width:, :], preferred_element_type=jnp.float32)
    out[...] = twist(state[:, :width], state[:, width:], t[...]).astype(out.dtype).reshape(out.shape)


def level(order, own, other, kernels, twiddles, index, bit, piece, whole=None, after=()):
    slots, laws, width = own.shape
    tiles = piece[1]
    tile = slots // tiles
    block = pl.BlockSpec((tile, laws, width), lambda i, o: (i, 0, 0))
    in_specs = [
        block,
        block,
        pl.BlockSpec((None, 2, 2, width, width), lambda i, o: (index, 0, 0, 0, 0)),
        pl.BlockSpec((None, None, tile, width), lambda i, o: (index + 1, *spot(i, piece), 0)),
    ]
    args, aliases = [own, other, kernels, twiddles], {}
    out_shape, out_spec = jax.ShapeDtypeStruct(own.shape, own.dtype), block
    if index == 2:
        out_shape = jax.ShapeDtypeStruct((*twiddles.shape[1:3], laws, width), own.dtype)
        out_spec = pl.BlockSpec((None, tile, laws, width), lambda i, o: (*spot(i, piece), 0, 0))
    if whole is not None:
        args.append(whole)
        in_specs.append(pl.BlockSpec(memory_space=pl.ANY))
        aliases = {5: 0}
    args += after
    in_specs += [pl.BlockSpec(memory_space=pl.ANY)] * len(after)
    return call(
        functools.partial(level_kernel, bit),
        out_shape,
        (tiles,),
        in_specs,
        out_spec,
        args,
        order,
        scratch=[pltpu.VMEM((2 * width, 2 * width), own.dtype)],
        aliases=aliases,
        cost=COST if index else (LCOST if piece[1] == PIECES[0] else 0),
        flops=8 * slots * laws * width * width,
        nbytes=6 * slots * laws * width,
    )


PLANE = (0, THIRD, FIRST, FIRST | THIRD)


def pack_kernel(*refs):
    blocks, factors, out = refs[:4], refs[4:8], refs[-1]
    for i, (w, t) in enumerate(zip(blocks, factors)):
        targets, slots, laws, width = w.shape
        rows = slots * laws
        for target in range(targets):
            block = twist_16(w[target].reshape(rows, width), t[0, target])
            out[i, target * rows : (target + 1) * rows, :] = block.astype(out.dtype)
            for later in range(2):
                start = targets * rows + (later * targets + target) * slots
                out[i, start : start + slots, :] = t[1 + later, target].astype(out.dtype)


def pack(weights, twiddles, far, after=()):
    _, slots, laws, width = weights.shape
    eighth = slots // 8
    rows = GATHERED * eighth * (laws + 2)

    def weights_of(place):
        return pl.BlockSpec((GATHERED, eighth, laws, width), lambda i: (0, my_place() ^ place, 0, 0))

    def factors_of(place):
        return pl.BlockSpec((3, GATHERED, eighth, width), lambda i: (0, 0, my_place() ^ place, 0))

    return call(
        pack_kernel,
        jax.ShapeDtypeStruct((4, rows, width), weights.dtype),
        (1,),
        [
            *[weights_of(place + far) for place in PLANE],
            *[factors_of(place + far) for place in PLANE],
            *[pl.BlockSpec(memory_space=pl.ANY)] * len(after),
        ],
        pl.BlockSpec((4, rows, width), lambda i: (0, 0, 0)),
        (*[weights] * 4, *[twiddles] * 4, *after),
        None,
        vmem=60 * 2**20 if far else VMEM,
        cost=NCOST,
        nbytes=16 * rows * width,
    )


def pair_kernel(order, near, far, *rest):
    outs = rest[-3:]
    for i, out in enumerate(outs):
        out[0] = near[i + 1]
        out[1] = far[i + 1]


def pair_up(order, near, far, after):
    _, rows, width = near.shape
    whole = pl.BlockSpec((4, rows, width), lambda i, o: (0, 0, 0))
    return call(
        pair_kernel,
        [jax.ShapeDtypeStruct((2, rows, width), near.dtype)] * 3,
        (1,),
        [whole, whole, *[pl.BlockSpec(memory_space=pl.ANY)] * len(after)],
        [pl.BlockSpec((2, rows, width), lambda i, o: (0, 0, 0))] * 3,
        (near, far, *after),
        order,
        nbytes=24 * rows * width,
    )


def gathered_kernel(laws, order, near, far, one, two, three, maps, *rest):
    *_, out_0, out_1, out_2, out_3, both = rest
    width = maps.shape[-1]
    outs = (out_0, out_1, out_2, out_3)
    slots = near.shape[1] // (laws + 2)
    for index, bit in enumerate((FIRST, SECOND, THIRD)):
        child = lax.div(order[0], bit) & 1
        for source in range(2):
            for goal in range(2):
                part = maps[index, child ^ goal, child ^ source]
                turned = roll_half(part.astype(jnp.float32)).astype(part.dtype)
                at = slice(source * width, (source + 1) * width)
                both[index, at, goal * width : (goal + 1) * width] = part
                both[index, at, (2 + goal) * width : (3 + goal) * width] = turned

    def piece(place, start, size):
        at = pl.ds(pl.multiple_of(start, 16), size)
        plane = PLANE.index(place & (FIRST | THIRD))
        if plane == 0:
            return (far if place & SECOND else near)[0, at, :]
        return (one, two, three)[plane - 1][1 if place & SECOND else 0, at, :]

    step_slots = 16

    def step(i, carry):
        rows = step_slots * laws
        values = [piece(place, i * rows, rows) for place in range(8)]
        for index, bit in enumerate((FIRST, SECOND, THIRD)):
            for place in range(8):
                if place & bit:
                    continue
                joint = jnp.concatenate([values[place], values[place | bit]], axis=1)
                state = jnp.dot(joint, both[index], preferred_element_type=jnp.float32)
                for goal in range(2):
                    mine = place | bit if goal else place
                    plain = state[:, goal * width : (goal + 1) * width]
                    if index < 2:
                        turned = state[:, (2 + goal) * width : (3 + goal) * width]
                        start = slots * laws + index * slots + i * step_slots
                        factors = piece(mine, start, step_slots).astype(jnp.float32)
                        values[mine] = twist(plain, turned, factors).astype(jnp.bfloat16)
                    else:
                        out = outs[PLANE.index(mine & (FIRST | THIRD))]
                        at = pl.ds(pl.multiple_of(i * rows, 16), rows)
                        out[1 if mine & SECOND else 0, at, :] = plain.astype(out.dtype)
        return carry

    lax.fori_loop(0, slots // step_slots, step, 0)


def gathered_levels(order, near, far, received, kernels, laws, after):
    _, rows, width = near.shape
    full = rows // (laws + 2) * laws
    first = pl.BlockSpec((1, rows, width), lambda i, o: (0, 0, 0))
    pair = pl.BlockSpec((2, rows, width), lambda i, o: (0, 0, 0))
    return call(
        functools.partial(gathered_kernel, laws),
        [jax.ShapeDtypeStruct((2, full, width), near.dtype)] * 4,
        (1,),
        [
            *(first, first, pair, pair, pair),
            pl.BlockSpec(kernels.shape, lambda i, o: (0, 0, 0, 0, 0)),
            *[pl.BlockSpec(memory_space=pl.ANY)] * len(after),
        ],
        [pl.BlockSpec((2, full, width), lambda i, o: (0, 0, 0))] * 4,
        (near, far, *received, kernels, *after),
        order,
        scratch=[pltpu.VMEM((3, 2 * width, 4 * width), near.dtype)],
        flops=3 * 8 * full * 4 * width * width,
        nbytes=32 * full * width,
    )


def far_kernel(order, a, b, c, d, *rest):
    out = rest[-1]
    for i, block in enumerate((a, b, c, d)):
        out[i] = block[0]


def far_part(order, blocks, after):
    _, rows, width = blocks[0].shape
    return call(
        far_kernel,
        jax.ShapeDtypeStruct((4, rows, width), blocks[0].dtype),
        (1,),
        [*[pl.BlockSpec((1, rows, width), lambda i, o: (1, 0, 0))] * 4, *[pl.BlockSpec(memory_space=pl.ANY)] * len(after)],
        pl.BlockSpec((4, rows, width), lambda i, o: (0, 0, 0)),
        (*blocks, *after),
        order,
        nbytes=16 * rows * width,
    )


def unpack_kernel(far, order, *refs):
    blocks, factors, (out, ready, done) = refs[:-8], refs[-8:-4], refs[-3:]
    copies = []
    for i, (place, t) in enumerate(zip(PLANE, factors)):
        targets, slots, laws, width = ready.shape[1:]
        rows = slots * laws
        state = blocks[0][i] if len(blocks) == 1 else blocks[i][0]
        for target in range(targets):
            block = twist_16(state[target * rows : (target + 1) * rows, :], t[target])
            ready[i, target] = block.astype(out.dtype).reshape(slots, laws, width)
        at = pl.ds(pl.multiple_of(order[place + far] * slots, slots), slots)
        copies.append(pltpu.make_async_copy(ready.at[i], out.at[pl.ds(0, targets), at], done.at[i]))
        copies[-1].start()
    for copy in copies:
        copy.wait()


def unpack(order, blocks, twiddles, whole, far):
    _, slots, laws, width = whole.shape
    eighth = slots // 8
    rows = GATHERED * eighth * laws

    def factors_of(place):
        return pl.BlockSpec((None, GATHERED, eighth, width), lambda i, o: (3, 0, o[place], 0))

    count = 4 // len(blocks)
    return call(
        functools.partial(unpack_kernel, far),
        jax.ShapeDtypeStruct(whole.shape, whole.dtype),
        (1,),
        [
            *[pl.BlockSpec((count, rows, width), lambda i, o: (0, 0, 0))] * len(blocks),
            *[factors_of(place + far) for place in PLANE],
            pl.BlockSpec(memory_space=pl.ANY),
        ],
        pl.BlockSpec(memory_space=pl.ANY),
        (*blocks, *[twiddles] * 4, whole),
        order,
        scratch=[pltpu.VMEM((4, GATHERED, eighth, laws, width), whole.dtype), pltpu.SemaphoreType.DMA((4,))],
        aliases={len(blocks) + 5: 0},
        nbytes=16 * rows * width,
    )


def body(weights_in, twiddles, kernels):
    targets, slots, laws, _ = weights_in.shape
    order = my_order()
    far_send = pack(weights_in, twiddles, SECOND)
    far = swap(far_send, SECOND)
    near = pack(weights_in, twiddles, 0, [far_send])
    cuts = pieces(targets, slots)
    own, after = [None] * len(cuts), far_send
    for i in FIRST_ORDER:
        own[i] = after = first_twist(order, weights_in, twiddles, cuts[i], after)
    other = [swap(block, FIRST) for block in own]
    first, after = [None] * len(cuts), []
    for i in LEVEL_ORDER:
        first[i] = level(order, own[i], other[i], kernels, twiddles, 0, FIRST, cuts[i], None, after)
        after = [first[i]]
    own = first

    def next_level(index, bit, own, other):
        return [level(order, *pair, kernels, twiddles, index, bit, piece) for *pair, piece in zip(own, other, cuts)]

    pairs = pair_up(order, near, far, own)
    received = [swap(pair, place) for pair, place in zip(pairs, PLANE[1:])]
    own = next_level(1, SECOND, own, [swap(block, SECOND) for block in own])
    other = [swap(block, THIRD) for block in own]
    whole = level(order, own[0], other[0], kernels, twiddles, 2, THIRD, cuts[0])
    done = gathered_levels(order, near, far, received, kernels, laws, own[:1])
    back = [done[0], *[swap(block, place) for block, place in zip(done[1:], PLANE[1:])]]
    far_back = swap(far_part(order, back, [own[-2], whole]), SECOND)
    for *pair, piece in list(zip(own, other, cuts))[1:]:
        whole = level(order, *pair, kernels, twiddles, 2, THIRD, piece, whole)
    whole = unpack(order, back, twiddles, whole, 0)
    return unpack(order, [far_back], twiddles, whole, SECOND)


def solution(mesh):
    return jax.shard_map(
        body,
        mesh=mesh,
        in_specs=(P(None, ("src", "tgt"), None, None), P(None, None, ("src", "tgt"), None), P()),
        out_specs=P(None, ("src", "tgt"), None, None),
        check_vma=False,
    )
```

```python
import functools

import jax
import jax.numpy as jnp
from jax import lax
from jax.experimental import pallas as pl
from jax.experimental.pallas import tpu as pltpu
from jax.sharding import PartitionSpec as P

FIRST, SECOND, THIRD = 4, 2, 1
GATHERED = 2
PIECES = (2, 3, 3)
FIRST_ORDER = (0, 1, 2)
LEVEL_ORDER = (0, 1, 2)
COST = 4
TCOST = 0
LCOST = 12
NCOST = 4
VMEM = 48 * 2**20


def swap(block, mask):
    n_src, n_tgt = lax.axis_size("src"), lax.axis_size("tgt")
    flip_src = (n_src // 2 if mask & FIRST else 0) + (n_src // 4 if mask & SECOND else 0)
    flip_tgt = n_tgt // 2 if mask & THIRD else 0
    if not flip_tgt:
        return lax.ppermute(block, "src", [(i, i ^ flip_src) for i in range(n_src)])
    if not flip_src:
        return lax.ppermute(block, "tgt", [(i, i ^ flip_tgt) for i in range(n_tgt)])
    route = []
    for i in range(n_src):
        for j in range(n_tgt):
            route.append((i * n_tgt + j, (i ^ flip_src) * n_tgt + (j ^ flip_tgt)))
    return lax.ppermute(block, ("src", "tgt"), route)


def my_place():
    n_src, n_tgt = lax.axis_size("src"), lax.axis_size("tgt")
    return lax.div(lax.axis_index("src"), n_src // 4) * 2 + lax.div(lax.axis_index("tgt"), n_tgt // 2)


def my_order():
    return jnp.bitwise_xor(my_place().astype(jnp.int32), jnp.arange(8, dtype=jnp.int32))


def roll_half(block):
    return pltpu.roll(block, block.shape[-1] // 2, 1)


def phases(rows):
    turned = roll_half(rows)
    low = lax.broadcasted_iota(jnp.int32, rows.shape, 1) < rows.shape[-1] // 2
    return jnp.where(low, rows, turned)[:, None, :], jnp.where(low, -turned, rows)[:, None, :]


def twist(plain, turned, rows):
    co, si = phases(rows)
    shape = (rows.shape[0], plain.shape[0] // rows.shape[0], plain.shape[1])
    return (plain.reshape(shape) * co + turned.reshape(shape) * si).reshape(plain.shape)


def twist_16(block, rows):
    width = block.shape[-1]
    row = lax.broadcasted_iota(jnp.int32, (width, width), 0)
    column = lax.broadcasted_iota(jnp.int32, (width, width), 1)
    exchange = (jnp.abs(row - column) == width // 2).astype(jnp.float32).astype(block.dtype)
    turned = jnp.dot(block, exchange, preferred_element_type=jnp.float32)
    return twist(block.astype(jnp.float32), turned, rows)


def call(kernel, out_shape, grid, in_specs, out_specs, args, order, scratch=(), aliases=None, vmem=VMEM, cost=COST, flops=0, nbytes=0):
    known = () if order is None else (order,)
    return pl.pallas_call(
        kernel,
        out_shape=out_shape,
        grid_spec=pltpu.PrefetchScalarGridSpec(
            num_scalar_prefetch=len(known), grid=grid, in_specs=in_specs, out_specs=out_specs, scratch_shapes=list(scratch)
        ),
        input_output_aliases=aliases or {},
        compiler_params=pltpu.CompilerParams(vmem_limit_bytes=vmem),
        cost_estimate=pl.CostEstimate(flops=cost * flops, bytes_accessed=cost * nbytes, transcendentals=0),
    )(*known, *args)


def pieces(targets, slots):
    per_target = sum(PIECES) // (targets - GATHERED)
    starts = [GATHERED * per_target + sum(PIECES[:i]) for i in range(len(PIECES))]
    return [(start, count, per_target) for start, count in zip(starts, PIECES)]


def spot(i, piece):
    start, _, per_target = piece
    return lax.div(start + i, per_target), lax.rem(start + i, per_target)


def first_kernel(order, w, t, _, out):
    slots, laws, width = out.shape
    out[...] = twist_16(w[...].reshape(slots * laws, width), t[...]).astype(out.dtype).reshape(out.shape)


def first_twist(order, weights, twiddles, piece, after):
    _, slots, laws, width = weights.shape
    tile, tiles = slots // piece[2], piece[1]
    return call(
        first_kernel,
        jax.ShapeDtypeStruct((tiles * tile, laws, width), weights.dtype),
        (tiles,),
        [
            pl.BlockSpec((None, tile, laws, width), lambda i, o: (*spot(i, piece), 0, 0)),
            pl.BlockSpec((None, None, tile, width), lambda i, o: (0, *spot(i, piece), 0)),
            pl.BlockSpec(memory_space=pl.ANY),
        ],
        pl.BlockSpec((tile, laws, width), lambda i, o: (i, 0, 0)),
        (weights, twiddles, after),
        order,
        cost=TCOST,
        nbytes=4 * tiles * tile * laws * width,
    )


def level_kernel(bit, order, own, other, maps, t, *rest):
    out, both = rest[-2:]
    slots, laws, width = own.shape

    @pl.when(pl.program_id(0) == 0)
    def _():
        child = lax.div(order[0], bit) & 1
        for source in range(2):
            part = maps[child, child if source == 0 else 1 - child]
            both[source * width : (source + 1) * width, :width] = part
            turned = roll_half(part.astype(jnp.float32)).astype(part.dtype)
            both[source * width : (source + 1) * width, width:] = turned

    rows = slots * laws
    state = jnp.dot(own[...].reshape(rows, width), both[:width, :], preferred_element_type=jnp.float32)
    state += jnp.dot(other[...].reshape(rows, width), both[width:, :], preferred_element_type=jnp.float32)
    out[...] = twist(state[:, :width], state[:, width:], t[...]).astype(out.dtype).reshape(out.shape)


def level(order, own, other, kernels, twiddles, index, bit, piece, whole=None, after=()):
    slots, laws, width = own.shape
    tiles = piece[1]
    tile = slots // tiles
    block = pl.BlockSpec((tile, laws, width), lambda i, o: (i, 0, 0))
    in_specs = [
        block,
        block,
        pl.BlockSpec((None, 2, 2, width, width), lambda i, o: (index, 0, 0, 0, 0)),
        pl.BlockSpec((None, None, tile, width), lambda i, o: (index + 1, *spot(i, piece), 0)),
    ]
    args, aliases = [own, other, kernels, twiddles], {}
    out_shape, out_spec = jax.ShapeDtypeStruct(own.shape, own.dtype), block
    if index == 2:
        out_shape = jax.ShapeDtypeStruct((*twiddles.shape[1:3], laws, width), own.dtype)
        out_spec = pl.BlockSpec((None, tile, laws, width), lambda i, o: (*spot(i, piece), 0, 0))
    if whole is not None:
        args.append(whole)
        in_specs.append(pl.BlockSpec(memory_space=pl.ANY))
        aliases = {5: 0}
    args += after
    in_specs += [pl.BlockSpec(memory_space=pl.ANY)] * len(after)
    return call(
        functools.partial(level_kernel, bit),
        out_shape,
        (tiles,),
        in_specs,
        out_spec,
        args,
        order,
        scratch=[pltpu.VMEM((2 * width, 2 * width), own.dtype)],
        aliases=aliases,
        cost=COST if index else (LCOST if piece[1] == PIECES[0] else 0),
        flops=8 * slots * laws * width * width,
        nbytes=6 * slots * laws * width,
    )


PLANE = (0, THIRD, FIRST, FIRST | THIRD)


def pack_kernel(*refs):
    blocks, factors, (whole, out, done) = refs[:4], refs[4:8], refs[-3:]
    copies = []
    for i, (w, t) in enumerate(zip(blocks, factors)):
        targets, slots, laws, width = w.shape
        rows = slots * laws
        for target in range(targets):
            block = twist_16(w[target].reshape(rows, width), t[0, target])
            out[i, target * rows : (target + 1) * rows, :] = block.astype(out.dtype)
            for later in range(2):
                start = targets * rows + (later * targets + target) * slots
                out[i, start : start + slots, :] = t[1 + later, target].astype(out.dtype)
        copies.append(pltpu.make_async_copy(out.at[i], whole.at[i], done.at[i]))
        copies[-1].start()
    for copy in copies:
        copy.wait()


def pack(weights, twiddles, far, after=()):
    _, slots, laws, width = weights.shape
    eighth = slots // 8
    rows = GATHERED * eighth * (laws + 2)

    def weights_of(place):
        return pl.BlockSpec((GATHERED, eighth, laws, width), lambda i: (0, my_place() ^ place, 0, 0))

    def factors_of(place):
        return pl.BlockSpec((3, GATHERED, eighth, width), lambda i: (0, 0, my_place() ^ place, 0))

    return call(
        pack_kernel,
        jax.ShapeDtypeStruct((4, rows, width), weights.dtype),
        (1,),
        [
            *[weights_of(place + far) for place in PLANE],
            *[factors_of(place + far) for place in PLANE],
            *[pl.BlockSpec(memory_space=pl.ANY)] * len(after),
        ],
        pl.BlockSpec(memory_space=pl.ANY),
        (*[weights] * 4, *[twiddles] * 4, *after),
        None,
        scratch=[pltpu.VMEM((4, rows, width), weights.dtype), pltpu.SemaphoreType.DMA((4,))],
        vmem=60 * 2**20 if far else VMEM,
        cost=NCOST,
        nbytes=16 * rows * width,
    )


def pair_kernel(order, near, far, *rest):
    outs = rest[-3:]
    for i, out in enumerate(outs):
        out[0] = near[i + 1]
        out[1] = far[i + 1]


def pair_up(order, near, far, after):
    _, rows, width = near.shape
    whole = pl.BlockSpec((4, rows, width), lambda i, o: (0, 0, 0))
    return call(
        pair_kernel,
        [jax.ShapeDtypeStruct((2, rows, width), near.dtype)] * 3,
        (1,),
        [whole, whole, *[pl.BlockSpec(memory_space=pl.ANY)] * len(after)],
        [pl.BlockSpec((2, rows, width), lambda i, o: (0, 0, 0))] * 3,
        (near, far, *after),
        order,
        nbytes=24 * rows * width,
    )


def gathered_kernel(laws, order, near, far, one, two, three, maps, *rest):
    *_, out_0, out_1, out_2, out_3, both = rest
    width = maps.shape[-1]
    outs = (out_0, out_1, out_2, out_3)
    slots = near.shape[1] // (laws + 2)
    for index, bit in enumerate((FIRST, SECOND, THIRD)):
        child = lax.div(order[0], bit) & 1
        for source in range(2):
            for goal in range(2):
                part = maps[index, child ^ goal, child ^ source]
                turned = roll_half(part.astype(jnp.float32)).astype(part.dtype)
                at = slice(source * width, (source + 1) * width)
                both[index, at, goal * width : (goal + 1) * width] = part
                both[index, at, (2 + goal) * width : (3 + goal) * width] = turned

    def piece(place, start, size):
        at = pl.ds(pl.multiple_of(start, 16), size)
        plane = PLANE.index(place & (FIRST | THIRD))
        if plane == 0:
            return (far if place & SECOND else near)[0, at, :]
        return (one, two, three)[plane - 1][1 if place & SECOND else 0, at, :]

    step_slots = 16

    def step(i, carry):
        rows = step_slots * laws
        values = [piece(place, i * rows, rows) for place in range(8)]
        for index, bit in enumerate((FIRST, SECOND, THIRD)):
            for place in range(8):
                if place & bit:
                    continue
                joint = jnp.concatenate([values[place], values[place | bit]], axis=1)
                state = jnp.dot(joint, both[index], preferred_element_type=jnp.float32)
                for goal in range(2):
                    mine = place | bit if goal else place
                    plain = state[:, goal * width : (goal + 1) * width]
                    if index < 2:
                        turned = state[:, (2 + goal) * width : (3 + goal) * width]
                        start = slots * laws + index * slots + i * step_slots
                        factors = piece(mine, start, step_slots).astype(jnp.float32)
                        values[mine] = twist(plain, turned, factors).astype(jnp.bfloat16)
                    else:
                        out = outs[PLANE.index(mine & (FIRST | THIRD))]
                        at = pl.ds(pl.multiple_of(i * rows, 16), rows)
                        out[1 if mine & SECOND else 0, at, :] = plain.astype(out.dtype)
        return carry

    lax.fori_loop(0, slots // step_slots, step, 0)


def gathered_levels(order, near, far, received, kernels, laws, after):
    _, rows, width = near.shape
    full = rows // (laws + 2) * laws
    first = pl.BlockSpec((1, rows, width), lambda i, o: (0, 0, 0))
    pair = pl.BlockSpec((2, rows, width), lambda i, o: (0, 0, 0))
    return call(
        functools.partial(gathered_kernel, laws),
        [jax.ShapeDtypeStruct((2, full, width), near.dtype)] * 4,
        (1,),
        [
            *(first, first, pair, pair, pair),
            pl.BlockSpec(kernels.shape, lambda i, o: (0, 0, 0, 0, 0)),
            *[pl.BlockSpec(memory_space=pl.ANY)] * len(after),
        ],
        [pl.BlockSpec((2, full, width), lambda i, o: (0, 0, 0))] * 4,
        (near, far, *received, kernels, *after),
        order,
        scratch=[pltpu.VMEM((3, 2 * width, 4 * width), near.dtype)],
        flops=3 * 8 * full * 4 * width * width,
        nbytes=32 * full * width,
    )


def far_kernel(order, a, b, c, d, *rest):
    out = rest[-1]
    for i, block in enumerate((a, b, c, d)):
        out[i] = block[0]


def far_part(order, blocks, after):
    _, rows, width = blocks[0].shape
    return call(
        far_kernel,
        jax.ShapeDtypeStruct((4, rows, width), blocks[0].dtype),
        (1,),
        [*[pl.BlockSpec((1, rows, width), lambda i, o: (1, 0, 0))] * 4, *[pl.BlockSpec(memory_space=pl.ANY)] * len(after)],
        pl.BlockSpec((4, rows, width), lambda i, o: (0, 0, 0)),
        (*blocks, *after),
        order,
        nbytes=16 * rows * width,
    )


def unpack_kernel(far, order, *refs):
    blocks, factors, (out, ready, done) = refs[:-8], refs[-8:-4], refs[-3:]
    copies = []
    for i, (place, t) in enumerate(zip(PLANE, factors)):
        targets, slots, laws, width = ready.shape[1:]
        rows = slots * laws
        state = blocks[0][i] if len(blocks) == 1 else blocks[i][0]
        for target in range(targets):
            block = twist_16(state[target * rows : (target + 1) * rows, :], t[target])
            ready[i, target] = block.astype(out.dtype).reshape(slots, laws, width)
        at = pl.ds(pl.multiple_of(order[place + far] * slots, slots), slots)
        copies.append(pltpu.make_async_copy(ready.at[i], out.at[pl.ds(0, targets), at], done.at[i]))
        copies[-1].start()
    for copy in copies:
        copy.wait()


def unpack(order, blocks, twiddles, whole, far):
    _, slots, laws, width = whole.shape
    eighth = slots // 8
    rows = GATHERED * eighth * laws

    def factors_of(place):
        return pl.BlockSpec((None, GATHERED, eighth, width), lambda i, o: (3, 0, o[place], 0))

    count = 4 // len(blocks)
    return call(
        functools.partial(unpack_kernel, far),
        jax.ShapeDtypeStruct(whole.shape, whole.dtype),
        (1,),
        [
            *[pl.BlockSpec((count, rows, width), lambda i, o: (0, 0, 0))] * len(blocks),
            *[factors_of(place + far) for place in PLANE],
            pl.BlockSpec(memory_space=pl.ANY),
        ],
        pl.BlockSpec(memory_space=pl.ANY),
        (*blocks, *[twiddles] * 4, whole),
        order,
        scratch=[pltpu.VMEM((4, GATHERED, eighth, laws, width), whole.dtype), pltpu.SemaphoreType.DMA((4,))],
        aliases={len(blocks) + 5: 0},
        nbytes=16 * rows * width,
    )


def body(weights_in, twiddles, kernels):
    targets, slots, laws, _ = weights_in.shape
    order = my_order()
    far_send = pack(weights_in, twiddles, SECOND)
    far = swap(far_send, SECOND)
    near = pack(weights_in, twiddles, 0, [far_send])
    cuts = pieces(targets, slots)
    own, after = [None] * len(cuts), far_send
    for i in FIRST_ORDER:
        own[i] = after = first_twist(order, weights_in, twiddles, cuts[i], after)
    other = [swap(block, FIRST) for block in own]
    first, after = [None] * len(cuts), []
    for i in LEVEL_ORDER:
        first[i] = level(order, own[i], other[i], kernels, twiddles, 0, FIRST, cuts[i], None, after)
        after = [first[i]]
    own = first

    def next_level(index, bit, own, other):
        return [level(order, *pair, kernels, twiddles, index, bit, piece) for *pair, piece in zip(own, other, cuts)]

    pairs = pair_up(order, near, far, own)
    received = [swap(pair, place) for pair, place in zip(pairs, PLANE[1:])]
    own = next_level(1, SECOND, own, [swap(block, SECOND) for block in own])
    other = [swap(block, THIRD) for block in own]
    whole = level(order, own[0], other[0], kernels, twiddles, 2, THIRD, cuts[0])
    done = gathered_levels(order, near, far, received, kernels, laws, own[:1])
    back = [done[0], *[swap(block, place) for block, place in zip(done[1:], PLANE[1:])]]
    far_back = swap(far_part(order, back, [own[-2], whole]), SECOND)
    for *pair, piece in list(zip(own, other, cuts))[1:]:
        whole = level(order, *pair, kernels, twiddles, 2, THIRD, piece, whole)
    whole = unpack(order, back, twiddles, whole, 0)
    return unpack(order, [far_back], twiddles, whole, SECOND)


def solution(mesh):
    return jax.shard_map(
        body,
        mesh=mesh,
        in_specs=(P(None, ("src", "tgt"), None, None), P(None, None, ("src", "tgt"), None), P()),
        out_specs=P(None, ("src", "tgt"), None, None),
        check_vma=False,
    )
```
